32 devices in a mesh: blk: 32 (over z, y, x, core).
Axes of the slice: x: 2, y: 2, z: 4, core: 2. Of those that a mesh axis runs over, the one named last changes fastest.
Arguments:
- queries: bfloat16 [4096, 512], P('blk'), may hold values from -8 to 8
- key_vectors: bfloat16 [4096, 512], P('blk'), may hold values from -8 to 8
- node_feats: bfloat16 [4096, 512], P('blk'), may hold values from -6 to 6
- w_value: bfloat16 [512, 512], replicated, may hold values from -0.25 to 0.25
- w_out: bfloat16 [512, 512], replicated, may hold values from -0.25 to 0.25
- band_mask: int32 [4096, 640], P('blk'), may hold values 0 or 1
- expander_mask: int32 [4096, 128], P('blk'), may hold values 0 or 1
- partner: int32 [32], P('blk'), may hold values from 0 to 31, as said below
- out_grad: bfloat16 [4096, 512], P('blk'), may hold values from -6 to 6
Outputs:
- layer_out: bfloat16 [4096, 512], P('blk')
- query_grad: bfloat16 [4096, 512], P('blk')
- key_grad: bfloat16 [4096, 512], P('blk')
- feature_grad: bfloat16 [4096, 512], P('blk')
The draws below stay inside these ranges and needn't reach their ends.
Inputs may be any that keep to these rules, and one draw needn't show every extreme that they name: partner[i] is i XOR m for every block i, with one m of 1 to 31 shared by all blocks.
All inputs are finite; a program needn't handle non-finite values. No bound on the sum of `band_mask` or of `expander_mask` on one device may be relied on, other than what follows from the above.
Results may differ from the reference program's by a relative error of at most 0.007.
Values may be sent and summed in bfloat16 or wider, within the bound.
No kernel may reach another device: no remote copies, remote signals or barrier semaphores. Data moves between devices by JAX's collectives and lax.ppermute only.
A program may use at most 64 MiB of HBM per device.

```python
import math
import jax
import jax.numpy as jnp
from jax import lax

D = 512
HEADS = 8
BLOCK = 128
NODES = 4096
N_BLK = 32


def draw_queries(key, part):
    base = jax.random.truncated_normal(jax.random.fold_in(key, 21), -4.0, 4.0, (NODES, D))
    return base.astype(jnp.float32).astype(jnp.bfloat16)


def draw_key_vectors(key, part):
    base = jax.random.truncated_normal(jax.random.fold_in(key, 22), -4.0, 4.0, (NODES, D))
    return base.astype(jnp.float32).astype(jnp.bfloat16)


def draw_partner(key, part):
    chosen = jax.random.randint(jax.random.fold_in(key, 31), (), 1, N_BLK).astype(jnp.int32)
    return jnp.bitwise_xor(jnp.arange(N_BLK, dtype=jnp.int32), chosen).astype(jnp.int32)


def set_ends(values, own_key, low, high):
    longest = values.shape.index(max(values.shape))
    spots = []
    for shift in (0, 1):
        where = [jax.random.randint(jax.random.fold_in(own_key, axis), (), 0, length) for axis, length in enumerate(values.shape)]
        where[longest] = (where[longest] + shift) % values.shape[longest]
        spots.append(tuple(where))
    return values.at[spots[0]].set(low).at[spots[1]].set(high)


def level_of(key, extent, split, least, largest):
    level, own = 1.0, jax.random.fold_in(key, 6)
    for position, shards_of in split:
        draws = jnp.exp(jax.random.uniform(jax.random.fold_in(own, position), (shards_of,), jnp.float32, least / len(split), largest / len(split)))
        level = level * jnp.repeat(draws, extent[position] // shards_of).reshape([-1 if axis == position else 1 for axis in range(len(extent))])
    return level


def bell_draw(stream_key, dims, spread, bound, shards=(), kind=jnp.bfloat16):
    array = jax.random.normal(stream_key, dims, jnp.float32) * spread
    if len(shards) > 0:
        array = level_of(stream_key, dims, shards, -0.22, 0.18) * array
    return jnp.clip(array, min=-bound, max=bound).astype(kind)


def setup_inputs(seed: int = 0) -> dict:
    streams_of = jax.random.split(jax.random.key(seed), 10)
    queries = draw_queries(jax.random.fold_in(streams_of[9], 71), 0)
    key_vectors = draw_key_vectors(jax.random.fold_in(streams_of[9], 71), 0)
    node_feats = bell_draw(streams_of[2], (NODES, D), 1.0, 6.0, ((0, 32),))
    w_value = bell_draw(streams_of[3], (D, D), D ** -0.5, 0.25)
    w_out = bell_draw(streams_of[4], (D, D), D ** -0.5, 0.25)
    band_mask = set_ends((jax.random.randint(streams_of[5], (NODES, 5 * BLOCK), 0, 8) < 1).astype(jnp.int32), jax.random.fold_in(streams_of[5], 1), 0, 1)
    expander_mask = set_ends((jax.random.randint(streams_of[6], (NODES, BLOCK), 0, 4) < 1).astype(jnp.int32), jax.random.fold_in(streams_of[6], 1), 0, 1)
    partner = draw_partner(jax.random.fold_in(streams_of[9], 71), 0)
    out_grad = bell_draw(streams_of[8], (NODES, D), 1.0, 6.0, ((0, 32),))
    return dict(queries=queries, key_vectors=key_vectors, node_feats=node_feats, w_value=w_value, w_out=w_out, band_mask=band_mask, expander_mask=expander_mask, partner=partner, out_grad=out_grad)


def head_split(matrix):
    return matrix.astype(jnp.float32).reshape(matrix.shape[0], HEADS, D // HEADS)

def forced_edges(key_total):
    row_ids = lax.broadcasted_iota(jnp.int32, (BLOCK, key_total), 0)
    col_ids = lax.broadcasted_iota(jnp.int32, (BLOCK, key_total), 1)
    local_col = col_ids - 2 * BLOCK
    return (local_col == row_ids) | (local_col == jnp.bitwise_xor(row_ids, 1))

def reference(queries, key_vectors, node_feats, w_value, w_out, band_mask, expander_mask, partner, out_grad):
    scale = 1.0 / math.sqrt(D // HEADS)
    values = jnp.dot(node_feats, w_value, preferred_element_type=jnp.float32).astype(jnp.bfloat16)
    attn_grad = jnp.dot(out_grad, w_out.T, preferred_element_type=jnp.float32).astype(jnp.bfloat16)
    query_dev = queries.reshape(N_BLK, BLOCK, D)
    key_dev = key_vectors.reshape(N_BLK, BLOCK, D)
    value_dev = values.reshape(N_BLK, BLOCK, D)
    grad_dev = attn_grad.reshape(N_BLK, BLOCK, D)
    band_dev = band_mask.reshape(N_BLK, BLOCK, 5 * BLOCK)
    expander_dev = expander_mask.reshape(N_BLK, BLOCK, BLOCK)

    def forward_block(device):
        sources = jnp.stack([(device + shift_by) % N_BLK for shift_by in (-2, -1, 0, 1, 2)] + [partner[device]]).astype(jnp.int32)
        all_keys = key_dev[sources].reshape(6 * BLOCK, D)
        all_values = value_dev[sources].reshape(6 * BLOCK, D)
        allowed = (jnp.concatenate([band_dev[device], expander_dev[device]], 1) != 0) | forced_edges(6 * BLOCK)
        scores = jnp.einsum('rhd,khd->hrk', head_split(query_dev[device]), head_split(all_keys)) * scale
        row_max = lax.optimization_barrier(jnp.max(jnp.where(allowed[None], scores, -jnp.inf), axis=-1, keepdims=True))
        weights = jnp.where(allowed[None], jnp.exp(scores - row_max), 0.0)
        row_total = lax.optimization_barrier(jnp.sum(weights, axis=-1, keepdims=True))
        prob_full = weights / row_total
        prob_half = prob_full.astype(jnp.bfloat16)
        attended = jnp.einsum('hrk,khd->rhd', prob_half.astype(jnp.float32), head_split(all_values)).reshape(BLOCK, D).astype(jnp.bfloat16)
        grad_prob = jnp.einsum('rhd,khd->hrk', head_split(grad_dev[device]), head_split(all_values))
        row_delta = lax.optimization_barrier(jnp.sum(prob_full * grad_prob, axis=-1, keepdims=True))
        grad_score = (prob_full * (grad_prob - row_delta) * scale).astype(jnp.bfloat16)
        query_grad = jnp.einsum('hrk,khd->rhd', grad_score.astype(jnp.float32), head_split(all_keys)).reshape(BLOCK, D).astype(jnp.bfloat16)
        return (attended, query_grad, row_max, row_total, row_delta)
    attended, query_grad, row_max, row_total, row_delta = lax.map(forward_block, jnp.arange(N_BLK, dtype=jnp.int32))

    def key_block(device):
        key_rows = key_dev[device]
        value_rows = value_dev[device]

        def partials(source, allowed):
            scores = jnp.einsum('rhd,khd->hrk', head_split(query_dev[source]), head_split(key_rows)) * scale
            prob_full = jnp.where(allowed[None], jnp.exp(scores - row_max[source]), 0.0) / row_total[source]
            prob_half = prob_full.astype(jnp.bfloat16)
            grad_prob = jnp.einsum('rhd,khd->hrk', head_split(grad_dev[source]), head_split(value_rows))
            grad_score = (prob_full * (grad_prob - row_delta[source]) * scale).astype(jnp.bfloat16)
            key_part = jnp.einsum('hrk,rhd->khd', grad_score.astype(jnp.float32), head_split(query_dev[source])).reshape(BLOCK, D).astype(jnp.bfloat16)
            value_part = jnp.einsum('hrk,rhd->khd', prob_half.astype(jnp.float32), head_split(grad_dev[source])).reshape(BLOCK, D).astype(jnp.bfloat16)
            return (key_part.astype(jnp.float32), value_part.astype(jnp.float32))
        key_sum = jnp.zeros((BLOCK, D), jnp.float32)
        value_sum = jnp.zeros((BLOCK, D), jnp.float32)
        for slot, shift_by in enumerate((-2, -1, 0, 1, 2)):
            source = ((device - shift_by) % N_BLK).astype(jnp.int32)
            allowed = band_dev[source][:, slot * BLOCK:(slot + 1) * BLOCK] != 0
            if slot == 2:
                allowed = allowed | forced_edges(BLOCK + 2 * BLOCK)[:, 2 * BLOCK:]
            key_part, value_part = partials(source, allowed)
            key_sum = key_sum + key_part
            value_sum = value_sum + value_part
        source = partner[device].astype(jnp.int32)
        key_part, value_part = partials(source, expander_dev[source] != 0)
        key_sum = key_sum + key_part
        value_sum = value_sum + value_part
        return (key_sum.astype(jnp.bfloat16), value_sum.astype(jnp.bfloat16))
    key_grad, value_grad = lax.map(key_block, jnp.arange(N_BLK, dtype=jnp.int32))
    attended = attended.reshape(NODES, D)
    layer_out = jnp.dot(attended, w_out, preferred_element_type=jnp.float32).astype(jnp.bfloat16)
    value_grad = value_grad.reshape(NODES, D)
    feature_grad = jnp.dot(value_grad, w_value.T, preferred_element_type=jnp.float32).astype(jnp.bfloat16)
    return (layer_out, query_grad.reshape(NODES, D), key_grad.reshape(NODES, D), feature_grad)
```

```python
from functools import partial

import jax
import jax.numpy as jnp
from jax import lax
from jax.experimental import pallas as pl
from jax.experimental.pallas import tpu as pltpu
from jax.sharding import PartitionSpec as P

HEADS = 8
ROLES = 6
OUTER, NEAR, OWN, TWIN, INNER, MATCH = range(ROLES)
GROUP_BITS = 5
BF16 = jnp.bfloat16
F32 = jnp.float32


def dot_nn(a, b):
    return lax.dot_general(a, b, (((1,), (0,)), ((), ())), preferred_element_type=F32)


def dot_nt(a, b):
    return lax.dot_general(a, b, (((1,), (1,)), ((), ())), preferred_element_type=F32)


def attend_kernel(
    side_ref, q_ref, g_ref, wv_ref, wo_ref, band_ref, exp_ref,
    outer_ref, near_ref, own_ref, twin_ref, inner_ref, match_ref,
    out_ref, dq_ref, d_outer, d_near, d_own, d_twin, d_inner, d_match,
    val_ref, bias_ref, qt_ref, gt_ref, ag_ref, qs_ref, att_ref,
):
    rows, width = q_ref.shape
    head = width // HEADS
    pair = 2 * head
    pairs = HEADS // 2
    sources = (outer_ref, near_ref, own_ref, twin_ref, inner_ref, match_ref)
    targets = (d_outer, d_near, d_own, d_twin, d_inner, d_match)
    side = side_ref[0]

    for role, ref in enumerate(sources):
        val_ref[pl.ds(role * rows, rows), :] = dot_nn(ref[rows:, :], wv_ref[...]).astype(BF16)

    ag = dot_nt(g_ref[...], wo_ref[...])
    ag_ref[...] = ag.astype(BF16)
    gt_ref[...] = ag.T.astype(BF16)
    scaled = q_ref[...].astype(F32) * (1.0 / 8.0)
    qs_ref[...] = scaled.astype(BF16)
    qt_ref[...] = scaled.T.astype(BF16)

    row_ids = lax.broadcasted_iota(jnp.int32, (rows, rows), 0)
    col_ids = lax.broadcasted_iota(jnp.int32, (rows, rows), 1)
    forced = (col_ids == row_ids) | (col_ids == jnp.bitwise_xor(row_ids, 1))
    for role in range(ROLES):
        if role == MATCH:
            allowed = exp_ref[...] != 0
        else:
            slot = jnp.where(side == 0, role, 4 - role)
            allowed = band_ref[:, pl.ds(pl.multiple_of(slot * rows, rows), rows)] != 0
        if role == OWN:
            allowed = allowed | forced
        bias_ref[:, role * rows : (role + 1) * rows] = jnp.where(allowed, 0.0, -jnp.inf)

    lane = lax.broadcasted_iota(jnp.int32, (rows, pair), 1)
    low = lane < head
    sub = lax.broadcasted_iota(jnp.int32, (pair, rows), 0)
    top = sub < head

    def split_rows(block):
        zero = jnp.zeros_like(block)
        return jnp.concatenate([jnp.where(low, block, zero), jnp.where(low, zero, block)], 0)

    def split_cols(block):
        zero = jnp.zeros_like(block)
        return jnp.concatenate([jnp.where(top, block, zero), jnp.where(top, zero, block)], 1)

    def one_pair(index, carry):
        start = pl.multiple_of(index * pair, pair)
        cols = pl.ds(start, pair)
        keys = jnp.concatenate([ref[:rows, cols] for ref in sources], 0)
        vals = val_ref[:, cols]
        scores = dot_nt(split_rows(qs_ref[:, cols]), keys)
        bias = bias_ref[...]
        scores = scores + jnp.concatenate([bias, bias], 0)
        row_max = jnp.max(scores, axis=-1, keepdims=True)
        weights = jnp.exp(scores - row_max)
        row_total = jnp.sum(weights, axis=-1, keepdims=True)
        prob = weights * (1.0 / row_total)
        half = prob.astype(BF16)
        grad_prob = dot_nt(split_rows(ag_ref[:, cols]), vals)
        delta = jnp.sum(prob * grad_prob, axis=-1, keepdims=True)
        grad_score = (prob * (grad_prob - delta)).astype(BF16)
        att = dot_nn(half, vals)
        att_ref[:, cols] = jnp.where(low, att[:rows], att[rows:]).astype(BF16)
        dq = dot_nn(grad_score, keys)
        dq_ref[:, cols] = (jnp.where(low, dq[:rows], dq[rows:]) * (1.0 / 8.0)).astype(BF16)
        dkt = dot_nn(split_cols(qt_ref[cols, :]), grad_score).astype(BF16)
        dvt = dot_nn(split_cols(gt_ref[cols, :]), half).astype(BF16)
        for role, ref in enumerate(targets):
            ref[cols, :] = dkt[:, role * rows : (role + 1) * rows]
            ref[pl.ds(pl.multiple_of(width + start, pair), pair), :] = dvt[
                :, role * rows : (role + 1) * rows
            ]
        return carry

    lax.fori_loop(0, pairs, one_pair, 0)
    out_ref[...] = dot_nn(att_ref[...], wo_ref[...]).astype(BF16)


def attend(side, q, g, wv, wo, band, expander, sources):
    rows, width = q.shape
    keys = ROLES * rows
    vmem = pl.BlockSpec(memory_space=pltpu.VMEM)
    piece = jax.ShapeDtypeStruct((2 * width, rows), BF16)
    return pl.pallas_call(
        attend_kernel,
        out_shape=[jax.ShapeDtypeStruct((rows, width), BF16)] * 2 + [piece] * ROLES,
        in_specs=[pl.BlockSpec(memory_space=pltpu.SMEM)] + [vmem] * (6 + ROLES),
        out_specs=[vmem] * (2 + ROLES),
        scratch_shapes=[
            pltpu.VMEM((keys, width), BF16),
            pltpu.VMEM((rows, keys), F32),
            pltpu.VMEM((width, rows), BF16),
            pltpu.VMEM((width, rows), BF16),
            pltpu.VMEM((rows, width), BF16),
            pltpu.VMEM((rows, width), BF16),
            pltpu.VMEM((rows, width), BF16),
        ],
        compiler_params=pltpu.CompilerParams(vmem_limit_bytes=40 * 1024 * 1024),
        cost_estimate=pl.CostEstimate(
            flops=14 * rows * keys * width, bytes_accessed=6 << 20, transcendentals=rows * keys * HEADS
        ),
        name="attend",
    )(side, q, g, wv, wo, band, expander, *sources)


def finish_kernel(wv_ref, *refs):
    parts, (dk_ref, df_ref) = refs[:-2], refs[-2:]
    width = wv_ref.shape[0]
    total = parts[0][...].astype(F32)
    for ref in parts[1:]:
        total = total + ref[...].astype(F32)
    dk_ref[...] = total[:width].T.astype(BF16)
    dv = total[width:].T.astype(BF16)
    df_ref[...] = dot_nt(dv, wv_ref[...]).astype(BF16)


def finish(wv, parts):
    rows = parts[0].shape[1]
    width = wv.shape[0]
    vmem = pl.BlockSpec(memory_space=pltpu.VMEM)
    return pl.pallas_call(
        finish_kernel,
        out_shape=[jax.ShapeDtypeStruct((rows, width), BF16)] * 2,
        in_specs=[vmem] * (1 + len(parts)),
        out_specs=[vmem] * 2,
        compiler_params=pltpu.CompilerParams(vmem_limit_bytes=40 * 1024 * 1024),
        name="finish",
    )(wv, *parts)


def send(value, route):
    count = lax.axis_size("blk")
    return lax.ppermute(value, "blk", [(s, route(s, count)) for s in range(count)])


def twin_of(s, count):
    return s ^ 1


def up_even(s, count):
    return (s + 2 - 4 * (s & 1)) % count


def down_even(s, count):
    return (s - 2 + 4 * (s & 1)) % count


def match_by(mask):
    return lambda s, count: s ^ mask


def body(mask, last, side, q, key_feats, moved, g, wv, wo, band, expander):
    inner = send(key_feats, down_even)
    outer = send(key_feats, up_even)
    match = send(moved, match_by(mask)) if mask else moved
    twin = send(key_feats, twin_of)
    near = send(inner, twin_of)
    out, dq, d_outer, d_near, d_own, d_twin, d_inner, d_match = attend(
        side, q, g, wv, wo, band, expander, (outer, near, key_feats, twin, inner, match)
    )
    joined = send(d_near, twin_of)
    r_outer = send(d_outer, down_even)
    r_match = send(d_match, match_by(mask)) if mask else d_match
    r_twin = send(d_twin, twin_of)
    d_inner = (d_inner.astype(F32) + joined.astype(F32)).astype(BF16)
    r_inner = send(d_inner, up_even)
    parts = (d_own, r_twin, r_outer, r_inner)
    if last:
        dk, df = finish(wv, parts + (r_match,))
        return out, dq, dk, df
    return (out, dq, r_match) + parts


def route_group(value, number, shift, size):
    def by(mask):
        return lambda moved: send(moved, match_by(mask << shift)) if mask else moved

    return lax.switch(number, [by(mask) for mask in range(size)], value)


def shards(
    queries, key_vectors, node_feats, w_value, w_out, band_mask, expander_mask, partner, out_grad
):
    count = lax.axis_size("blk")
    bits = count.bit_length() - 1
    place = lax.axis_index("blk")
    side = jnp.reshape(place & 1, (1,)).astype(jnp.int32)
    match_mask = jnp.bitwise_xor(partner[0], place)
    key_feats = jnp.concatenate([key_vectors, node_feats], 0)
    first = bits if bits <= GROUP_BITS else GROUP_BITS - 2
    groups = []
    for shift in range(first, bits, GROUP_BITS):
        width = min(GROUP_BITS, bits - shift)
        number = jnp.bitwise_and(jnp.right_shift(match_mask, shift), (1 << width) - 1)
        groups.append((number, shift, 1 << width))
    moved = key_feats
    for group in groups:
        moved = route_group(moved, *group)
    last = not groups
    masks = range(1 if last else 0, 1 << first)
    number = jnp.bitwise_and(match_mask, (1 << first) - 1) - masks[0]
    results = lax.switch(
        number,
        [partial(body, mask, last) for mask in masks],
        side, queries, key_feats, moved, out_grad, w_value, w_out, band_mask, expander_mask,
    )
    if last:
        return tuple(results)
    out, dq, returned = results[:3]
    for group in groups:
        returned = route_group(returned, *group)
    dk, df = finish(w_value, tuple(results[3:]) + (returned,))
    return out, dq, dk, df


def solution(mesh):
    split = P("blk", None)
    return jax.shard_map(
        shards,
        mesh=mesh,
        in_specs=(split, split, split, P(), P(), split, split, P("blk"), split),
        out_specs=(split, split, split, split),
        check_vma=False,
    )
```

```python
from functools import partial

import jax
import jax.numpy as jnp
from jax import lax
from jax.experimental import pallas as pl
from jax.experimental.pallas import tpu as pltpu
from jax.sharding import PartitionSpec as P

HEADS = 8
ROLES = 6
OUTER, NEAR, OWN, TWIN, INNER, MATCH = range(ROLES)
GROUP_BITS = 5
BF16 = jnp.bfloat16
F32 = jnp.float32


def dot_nn(a, b):
    return lax.dot_general(a, b, (((1,), (0,)), ((), ())), preferred_element_type=F32)


def dot_nt(a, b):
    return lax.dot_general(a, b, (((1,), (1,)), ((), ())), preferred_element_type=F32)


def attend_kernel(
    side_ref, q_ref, g_ref, wv_ref, wo_ref, band_ref, exp_ref,
    outer_ref, near_ref, own_ref, twin_ref, inner_ref, match_ref,
    out_ref, dq_ref, d_outer, d_near, d_own, d_twin, d_inner, d_match,
    val_ref, bias_ref, qt_ref, gt_ref, ag_ref, qs_ref, att_ref,
):
    rows, width = q_ref.shape
    head = width // HEADS
    pair = 2 * head
    pairs = HEADS // 2
    sources = (outer_ref, near_ref, own_ref, twin_ref, inner_ref, match_ref)
    targets = (d_outer, d_near, d_own, d_twin, d_inner, d_match)
    side = side_ref[0]

    for role, ref in enumerate(sources):
        val_ref[pl.ds(role * rows, rows), :] = dot_nn(ref[rows:, :], wv_ref[...]).astype(BF16)

    ag = dot_nt(g_ref[...], wo_ref[...])
    ag_ref[...] = ag.astype(BF16)
    gt_ref[...] = ag.T.astype(BF16)
    scaled = q_ref[...].astype(F32) * (1.0 / 8.0)
    qs_ref[...] = scaled.astype(BF16)
    qt_ref[...] = scaled.T.astype(BF16)

    row_ids = lax.broadcasted_iota(jnp.int32, (rows, rows), 0)
    col_ids = lax.broadcasted_iota(jnp.int32, (rows, rows), 1)
    forced = (col_ids == row_ids) | (col_ids == jnp.bitwise_xor(row_ids, 1))
    for role in range(ROLES):
        if role == MATCH:
            allowed = exp_ref[...] != 0
        else:
            slot = jnp.where(side == 0, role, 4 - role)
            allowed = band_ref[:, pl.ds(pl.multiple_of(slot * rows, rows), rows)] != 0
        if role == OWN:
            allowed = allowed | forced
        bias_ref[:, role * rows : (role + 1) * rows] = jnp.where(allowed, 0.0, -jnp.inf)

    lane = lax.broadcasted_iota(jnp.int32, (rows, pair), 1)
    low = lane < head
    sub = lax.broadcasted_iota(jnp.int32, (pair, rows), 0)
    top = sub < head

    def split_rows(block):
        zero = jnp.zeros_like(block)
        return jnp.concatenate([jnp.where(low, block, zero), jnp.where(low, zero, block)], 0)

    def split_cols(block):
        zero = jnp.zeros_like(block)
        return jnp.concatenate([jnp.where(top, block, zero), jnp.where(top, zero, block)], 1)

    def one_pair(index, carry):
        start = pl.multiple_of(index * pair, pair)
        cols = pl.ds(start, pair)
        keys = jnp.concatenate([ref[:rows, cols] for ref in sources], 0)
        vals = val_ref[:, cols]
        scores = dot_nt(split_rows(qs_ref[:, cols]), keys)
        bias = bias_ref[...]
        scores = scores + jnp.concatenate([bias, bias], 0)
        row_max = jnp.max(scores, axis=-1, keepdims=True)
        weights = jnp.exp(scores - row_max)
        row_total = jnp.sum(weights, axis=-1, keepdims=True)
        prob = weights * (1.0 / row_total)
        half = prob.astype(BF16)
        grad_prob = dot_nt(split_rows(ag_ref[:, cols]), vals)
        delta = jnp.sum(prob * grad_prob, axis=-1, keepdims=True)
        grad_score = (prob * (grad_prob - delta)).astype(BF16)
        att = dot_nn(half, vals)
        att_ref[:, cols] = jnp.where(low, att[:rows], att[rows:]).astype(BF16)
        dq = dot_nn(grad_score, keys)
        dq_ref[:, cols] = (jnp.where(low, dq[:rows], dq[rows:]) * (1.0 / 8.0)).astype(BF16)
        dkt = dot_nn(split_cols(qt_ref[cols, :]), grad_score).astype(BF16)
        dvt = dot_nn(split_cols(gt_ref[cols, :]), half).astype(BF16)
        for role, ref in enumerate(targets):
            ref[cols, :] = dkt[:, role * rows : (role + 1) * rows]
            ref[pl.ds(pl.multiple_of(width + start, pair), pair), :] = dvt[
                :, role * rows : (role + 1) * rows
            ]
        return carry

    lax.fori_loop(0, pairs, one_pair, 0)
    out_ref[...] = dot_nn(att_ref[...], wo_ref[...]).astype(BF16)


def attend(side, q, g, wv, wo, band, expander, sources):
    rows, width = q.shape
    keys = ROLES * rows
    vmem = pl.BlockSpec(memory_space=pltpu.VMEM)
    piece = jax.ShapeDtypeStruct((2 * width, rows), BF16)
    return pl.pallas_call(
        attend_kernel,
        out_shape=[jax.ShapeDtypeStruct((rows, width), BF16)] * 2 + [piece] * ROLES,
        in_specs=[pl.BlockSpec(memory_space=pltpu.SMEM)] + [vmem] * (6 + ROLES),
        out_specs=[vmem] * (2 + ROLES),
        scratch_shapes=[
            pltpu.VMEM((keys, width), BF16),
            pltpu.VMEM((rows, keys), F32),
            pltpu.VMEM((width, rows), BF16),
            pltpu.VMEM((width, rows), BF16),
            pltpu.VMEM((rows, width), BF16),
            pltpu.VMEM((rows, width), BF16),
            pltpu.VMEM((rows, width), BF16),
        ],
        compiler_params=pltpu.CompilerParams(vmem_limit_bytes=40 * 1024 * 1024),
        cost_estimate=pl.CostEstimate(
            flops=14 * rows * keys * width, bytes_accessed=6 << 20, transcendentals=rows * keys * HEADS
        ),
        name="attend",
    )(side, q, g, wv, wo, band, expander, *sources)


def finish_kernel(wv_ref, *refs):
    parts, (dk_ref, df_ref) = refs[:-2], refs[-2:]
    width = wv_ref.shape[0]
    total = parts[0][...].astype(F32)
    for ref in parts[1:]:
        total = total + ref[...].astype(F32)
    dk_ref[...] = total[:width].T.astype(BF16)
    dv = total[width:].T.astype(BF16)
    df_ref[...] = dot_nt(dv, wv_ref[...]).astype(BF16)


def finish(wv, parts):
    rows = parts[0].shape[1]
    width = wv.shape[0]
    vmem = pl.BlockSpec(memory_space=pltpu.VMEM)
    return pl.pallas_call(
        finish_kernel,
        out_shape=[jax.ShapeDtypeStruct((rows, width), BF16)] * 2,
        in_specs=[vmem] * (1 + len(parts)),
        out_specs=[vmem] * 2,
        compiler_params=pltpu.CompilerParams(vmem_limit_bytes=40 * 1024 * 1024),
        name="finish",
    )(wv, *parts)


def send(value, route):
    count = lax.axis_size("blk")
    return lax.ppermute(value, "blk", [(s, route(s, count)) for s in range(count)])


def twin_of(s, count):
    return s ^ 1


def up_even(s, count):
    return (s + 2 - 4 * (s & 1)) % count


def down_even(s, count):
    return (s - 2 + 4 * (s & 1)) % count


def match_by(mask):
    return lambda s, count: s ^ mask


def gather(mask, key_feats, moved):
    inner = send(key_feats, down_even)
    outer = send(key_feats, up_even)
    match = send(moved, match_by(mask)) if mask else moved
    twin = send(key_feats, twin_of)
    near = send(inner, twin_of)
    return outer, near, twin, inner, match


def scatter(mask, d_outer, d_near, d_twin, d_inner, d_match):
    joined = send(d_near, twin_of)
    outer = send(d_outer, down_even)
    match = send(d_match, match_by(mask)) if mask else d_match
    twin = send(d_twin, twin_of)
    d_inner = (d_inner.astype(F32) + joined.astype(F32)).astype(BF16)
    inner = send(d_inner, up_even)
    return twin, outer, inner, match


def route_group(value, number, shift, size):
    def by(mask):
        return lambda moved: send(moved, match_by(mask << shift)) if mask else moved

    return lax.switch(number, [by(mask) for mask in range(size)], value)


def shards(
    queries, key_vectors, node_feats, w_value, w_out, band_mask, expander_mask, partner, out_grad
):
    count = lax.axis_size("blk")
    bits = count.bit_length() - 1
    place = lax.axis_index("blk")
    side = jnp.reshape(place & 1, (1,)).astype(jnp.int32)
    match_mask = jnp.bitwise_xor(partner[0], place)
    key_feats = jnp.concatenate([key_vectors, node_feats], 0)
    first = min(bits, GROUP_BITS)
    groups = []
    for shift in range(first, bits, GROUP_BITS):
        width = min(GROUP_BITS, bits - shift)
        number = jnp.bitwise_and(jnp.right_shift(match_mask, shift), (1 << width) - 1)
        groups.append((number, shift, 1 << width))
    masks = range(0 if groups else 1, 1 << first)
    number = jnp.bitwise_and(match_mask, (1 << first) - 1) - masks[0]
    moved = key_feats
    for group in groups:
        moved = route_group(moved, *group)
    outer, near, twin, inner, match = lax.switch(
        number, [partial(gather, mask) for mask in masks], key_feats, moved
    )
    out, dq, d_outer, d_near, d_own, d_twin, d_inner, d_match = attend(
        side, queries, out_grad, w_value, w_out, band_mask, expander_mask,
        (outer, near, key_feats, twin, inner, match),
    )
    twin, outer, inner, match = lax.switch(
        number, [partial(scatter, mask) for mask in masks],
        d_outer, d_near, d_twin, d_inner, d_match,
    )
    for group in groups:
        match = route_group(match, *group)
    dk, df = finish(w_value, (d_own, twin, outer, inner, match))
    return out, dq, dk, df


def solution(mesh):
    split = P("blk", None)
    return jax.shard_map(
        shards,
        mesh=mesh,
        in_specs=(split, split, split, P(), P(), split, split, P("blk"), split),
        out_specs=(split, split, split, split),
        check_vma=False,
    )
```

```python
from functools import partial

import jax
import jax.numpy as jnp
from jax import lax
from jax.experimental import pallas as pl
from jax.experimental.pallas import tpu as pltpu
from jax.sharding import PartitionSpec as P

HEADS = 8
ROLES = 6
OWN, OUTER, NEAR, TWIN, INNER, MATCH = range(ROLES)
GROUP_BITS = 5
BF16 = jnp.bfloat16
F32 = jnp.float32
HBM = pl.BlockSpec(memory_space=pltpu.HBM)
VMEM = pl.BlockSpec(memory_space=pltpu.VMEM)
SMEM = pl.BlockSpec(memory_space=pltpu.SMEM)
LIMIT = pltpu.CompilerParams(vmem_limit_bytes=40 * 1024 * 1024)


def dot_nn(a, b):
    return lax.dot_general(a, b, (((1,), (0,)), ((), ())), preferred_element_type=F32)


def dot_nt(a, b):
    return lax.dot_general(a, b, (((1,), (1,)), ((), ())), preferred_element_type=F32)


def shape(*dims, kind=BF16):
    return jax.ShapeDtypeStruct(dims, kind)


def heads_kernel(*refs):
    side_ref, q_ref, g_ref, wo_ref, band_ref, exp_ref, own_ref = refs[:7]
    remote = refs[7 : 6 + ROLES]
    out_ref, dq_ref = refs[6 + ROLES : 8 + ROLES]
    targets = refs[8 + ROLES : 8 + 2 * ROLES]
    bias_ref, q2_ref, g2_ref, qt2_ref, gt2_ref, att_ref, landed, sems = refs[8 + 2 * ROLES :]
    rows, width = q_ref.shape
    head = width // HEADS
    pair = 2 * head
    pairs = HEADS // 2

    def arrival(place, index):
        cols = slice(index * pair, (index + 1) * pair)
        return pltpu.make_async_copy(
            remote[place].at[:, cols], landed.at[place, :, cols], sems.at[place, index]
        )

    for index in range(pairs):
        for place in range(ROLES - 1):
            arrival(place, index).start()

    side = side_ref[0]
    lane = lax.broadcasted_iota(jnp.int32, (rows, width), 1)
    low = jnp.bitwise_and(lane, head) == 0

    def spread(block, wide_ref, tall_ref):
        first = jnp.where(low, block, 0.0)
        second = jnp.where(low, 0.0, block)
        wide_ref[:rows, :] = first.astype(BF16)
        wide_ref[rows:, :] = second.astype(BF16)
        tall_ref[:, :rows] = first.T.astype(BF16)
        tall_ref[:, rows:] = second.T.astype(BF16)

    spread(q_ref[...].astype(F32) * (1.0 / 8.0), q2_ref, qt2_ref)
    grads = dot_nt(g_ref[...], wo_ref[...]).astype(BF16)
    spread(grads.astype(F32), g2_ref, gt2_ref)

    row_ids = lax.broadcasted_iota(jnp.int32, (rows, rows), 0)
    col_ids = lax.broadcasted_iota(jnp.int32, (rows, rows), 1)
    forced = (col_ids == row_ids) | (col_ids == jnp.bitwise_xor(row_ids, 1))
    for role, even_slot in ((OUTER, 0), (NEAR, 1), (OWN, 2), (TWIN, 3), (INNER, 4), (MATCH, None)):
        if role == MATCH:
            allowed = exp_ref[...] != 0
        else:
            slot = jnp.where(side == 0, even_slot, 4 - even_slot)
            allowed = band_ref[:, pl.ds(pl.multiple_of(slot * rows, rows), rows)] != 0
        if role == OWN:
            allowed = allowed | forced
        bias_ref[:, role * rows : (role + 1) * rows] = jnp.where(allowed, 0.0, -jnp.inf)

    low = low[:, :pair]
    for index in range(pairs):
        for place in range(ROLES - 1):
            arrival(place, index).wait()
        start = index * pair
        cols = slice(start, start + pair)
        keys = jnp.concatenate(
            [own_ref[:rows, cols]] + [landed[place, :rows, cols] for place in range(ROLES - 1)], 0
        )
        vals = jnp.concatenate(
            [own_ref[rows:, cols]] + [landed[place, rows:, cols] for place in range(ROLES - 1)], 0
        )
        bias = bias_ref[...]
        scores = dot_nt(q2_ref[:, cols], keys) + jnp.concatenate([bias, bias], 0)
        row_max = jnp.max(scores, axis=-1, keepdims=True)
        weights = jnp.exp(scores - row_max)
        row_total = jnp.sum(weights, axis=-1, keepdims=True)
        prob = weights * (1.0 / row_total)
        half = prob.astype(BF16)
        grad_prob = dot_nt(g2_ref[:, cols], vals)
        delta = jnp.sum(prob * grad_prob, axis=-1, keepdims=True)
        grad_score = (prob * (grad_prob - delta)).astype(BF16)
        att = dot_nn(half, vals)
        att_ref[:, cols] = jnp.where(low, att[:rows], att[rows:]).astype(BF16)
        dq = dot_nn(grad_score, keys)
        dq_ref[:, cols] = (jnp.where(low, dq[:rows], dq[rows:]) * (1.0 / 8.0)).astype(BF16)
        dkt = dot_nn(qt2_ref[cols, :], grad_score).astype(BF16)
        dvt = dot_nn(gt2_ref[cols, :], half).astype(BF16)
        for role, ref in enumerate(targets):
            ref[cols, :] = dkt[:, role * rows : (role + 1) * rows]
            ref[width + start : width + start + pair, :] = dvt[:, role * rows : (role + 1) * rows]
    out_ref[...] = dot_nn(att_ref[...], wo_ref[...]).astype(BF16)


def attend(side, q, g, wo, band, expander, own, remote):
    rows, width = q.shape
    return pl.pallas_call(
        heads_kernel,
        out_shape=[shape(rows, width)] * 2 + [shape(2 * width, rows)] * ROLES,
        in_specs=[SMEM] + [VMEM] * 6 + [HBM] * (ROLES - 1),
        out_specs=[VMEM] * (2 + ROLES),
        scratch_shapes=[
            pltpu.VMEM((rows, ROLES * rows), F32),
            pltpu.VMEM((2 * rows, width), BF16),
            pltpu.VMEM((2 * rows, width), BF16),
            pltpu.VMEM((width, 2 * rows), BF16),
            pltpu.VMEM((width, 2 * rows), BF16),
            pltpu.VMEM((rows, width), BF16),
            pltpu.VMEM((ROLES - 1, 2 * rows, width), BF16),
            pltpu.SemaphoreType.DMA((ROLES - 1, HEADS // 2)),
        ],
        compiler_params=LIMIT,
        name="heads",
    )(side, q, g, wo, band, expander, own, *remote)


def finish_kernel(wv_ref, own_ref, *refs):
    parts, (dk_ref, df_ref, landed, sems) = refs[:-4], refs[-4:]
    width, rows = wv_ref.shape[0], own_ref.shape[1]

    def arrival(place, half):
        span = slice(half * width, (half + 1) * width)
        return pltpu.make_async_copy(
            parts[place].at[span, :], landed.at[place, span, :], sems.at[place, half]
        )

    for half in (1, 0):
        for place in range(len(parts)):
            arrival(place, half).start()
    for half in (1, 0):
        span = slice(half * width, (half + 1) * width)
        total = own_ref[span, :].astype(F32)
        for place in range(len(parts)):
            arrival(place, half).wait()
            total = total + landed[place, span, :].astype(F32)
        total = total.T.astype(BF16)
        if half:
            df_ref[...] = dot_nt(total, wv_ref[...]).astype(BF16)
        else:
            dk_ref[...] = total


def finish(wv, own, parts):
    rows = own.shape[1]
    width = wv.shape[0]
    return pl.pallas_call(
        finish_kernel,
        out_shape=[shape(rows, width)] * 2,
        in_specs=[VMEM] * 2 + [HBM] * len(parts),
        out_specs=[VMEM] * 2,
        scratch_shapes=[
            pltpu.VMEM((len(parts), 2 * width, rows), BF16),
            pltpu.SemaphoreType.DMA((len(parts), 2)),
        ],
        compiler_params=LIMIT,
        name="finish",
    )(wv, own, *parts)


def send(value, route):
    count = lax.axis_size("blk")
    return lax.ppermute(value, "blk", [(s, route(s, count)) for s in range(count)])


def twin_of(s, count):
    return s ^ 1


def up_even(s, count):
    return (s + 2 - 4 * (s & 1)) % count


def down_even(s, count):
    return (s - 2 + 4 * (s & 1)) % count


def match_by(mask):
    return lambda s, count: s ^ mask


def gather(mask, key_vals, moved):
    inner = send(key_vals, down_even)
    outer = send(key_vals, up_even)
    match = send(moved, match_by(mask)) if mask else moved
    twin = send(key_vals, twin_of)
    near = send(inner, twin_of)
    return outer, near, twin, inner, match


def scatter(mask, d_outer, d_near, d_twin, d_inner, d_match):
    joined = send(d_near, twin_of)
    outer = send(d_outer, down_even)
    match = send(d_match, match_by(mask)) if mask else d_match
    twin = send(d_twin, twin_of)
    d_inner = (d_inner.astype(F32) + joined.astype(F32)).astype(BF16)
    inner = send(d_inner, up_even)
    return twin, outer, inner, match


def route_group(value, number, shift, size):
    def by(mask):
        return lambda moved: send(moved, match_by(mask << shift)) if mask else moved

    return lax.switch(number, [by(mask) for mask in range(size)], value)


def shards(
    queries, key_vectors, node_feats, w_value, w_out, band_mask, expander_mask, partner, out_grad
):
    count = lax.axis_size("blk")
    bits = count.bit_length() - 1
    place = lax.axis_index("blk")
    side = jnp.reshape(place & 1, (1,)).astype(jnp.int32)
    match_mask = jnp.bitwise_xor(partner[0], place)
    values = lax.dot_general(
        node_feats, w_value, (((1,), (0,)), ((), ())), preferred_element_type=F32
    ).astype(BF16)
    key_vals = jnp.concatenate([key_vectors, values], 0)
    first = min(bits, GROUP_BITS)
    groups = []
    for shift in range(first, bits, GROUP_BITS):
        width = min(GROUP_BITS, bits - shift)
        number = jnp.bitwise_and(jnp.right_shift(match_mask, shift), (1 << width) - 1)
        groups.append((number, shift, 1 << width))
    masks = range(0 if groups else 1, 1 << first)
    number = jnp.bitwise_and(match_mask, (1 << first) - 1) - masks[0]
    moved = key_vals
    for group in groups:
        moved = route_group(moved, *group)
    outer, near, twin, inner, match = lax.switch(
        number, [partial(gather, mask) for mask in masks], key_vals, moved
    )
    out, dq, d_own, d_outer, d_near, d_twin, d_inner, d_match = attend(
        side, queries, out_grad, w_out, band_mask, expander_mask,
        key_vals, (outer, near, twin, inner, match),
    )
    twin, outer, inner, match = lax.switch(
        number, [partial(scatter, mask) for mask in masks],
        d_outer, d_near, d_twin, d_inner, d_match,
    )
    for group in groups:
        match = route_group(match, *group)
    dk, df = finish(w_value, d_own, (twin, outer, inner, match))
    return out, dq, dk, df


def solution(mesh):
    split = P("blk", None)
    return jax.shard_map(
        shards,
        mesh=mesh,
        in_specs=(split, split, split, P(), P(), split, split, P("blk"), split),
        out_specs=(split, split, split, split),
        check_vma=False,
    )
```

```python
from functools import partial

import jax
import jax.numpy as jnp
from jax import lax
from jax.experimental import pallas as pl
from jax.experimental.pallas import tpu as pltpu
from jax.sharding import PartitionSpec as P

HEADS = 8
ROLES = 6
QUAD = 4
OWN, OUTER, NEAR, TWIN, INNER, MATCH = range(ROLES)
GROUP_BITS = 5
BF16 = jnp.bfloat16
F32 = jnp.float32
HBM = pl.BlockSpec(memory_space=pltpu.HBM)
VMEM = pl.BlockSpec(memory_space=pltpu.VMEM)
SMEM = pl.BlockSpec(memory_space=pltpu.SMEM)
LIMIT = pltpu.CompilerParams(vmem_limit_bytes=40 * 1024 * 1024)


def dot_nn(a, b):
    return lax.dot_general(a, b, (((1,), (0,)), ((), ())), preferred_element_type=F32)


def dot_nt(a, b):
    return lax.dot_general(a, b, (((1,), (1,)), ((), ())), preferred_element_type=F32)


def shape(*dims, kind=BF16):
    return jax.ShapeDtypeStruct(dims, kind)


def heads_kernel(*refs):
    side_ref, q_ref, g_ref, wo_ref, band_ref, exp_ref, own_ref = refs[:7]
    remote = refs[7 : 6 + ROLES]
    out_hbm, dq_hbm = refs[6 + ROLES : 8 + ROLES]
    targets = refs[8 + ROLES : 8 + 2 * ROLES]
    bias_ref, q2_ref, g2_ref, qt2_ref, gt2_ref, att_ref, landed, sems = refs[8 + 2 * ROLES : -3]
    out_ref, dq_ref, sink_sems = refs[-3:]
    rows, width = q_ref.shape
    head = width // HEADS
    pair = 2 * head

    def arrival(place, index):
        return pltpu.make_async_copy(remote[place], landed.at[place], sems.at[place, index])

    for place in range(ROLES - 1):
        arrival(place, 0).start()

    side = side_ref[0]
    lane = lax.broadcasted_iota(jnp.int32, (rows, width), 1)
    low = jnp.bitwise_and(lane, head) == 0
    quad_place = jnp.bitwise_and(lane, QUAD * head - 1) // head

    def spread(block, wide_ref, tall_ref):
        first = jnp.where(low, block, 0.0)
        second = jnp.where(low, 0.0, block)
        for member in range(QUAD):
            mine = quad_place == member
            wide_ref[member * rows : (member + 1) * rows, :] = jnp.where(mine, block, 0.0).astype(BF16)
        tall_ref[:, :rows] = first.T.astype(BF16)
        tall_ref[:, rows:] = second.T.astype(BF16)

    spread(q_ref[...].astype(F32) * (1.0 / 8.0), q2_ref, qt2_ref)
    grads = dot_nt(g_ref[...], wo_ref[...]).astype(BF16)
    spread(grads.astype(F32), g2_ref, gt2_ref)

    row_ids = lax.broadcasted_iota(jnp.int32, (rows, rows), 0)
    col_ids = lax.broadcasted_iota(jnp.int32, (rows, rows), 1)
    forced = (col_ids == row_ids) | (col_ids == jnp.bitwise_xor(row_ids, 1))
    for role, even_slot in ((OUTER, 0), (NEAR, 1), (OWN, 2), (TWIN, 3), (INNER, 4), (MATCH, None)):
        if role == MATCH:
            allowed = exp_ref[...] != 0
        else:
            slot = jnp.where(side == 0, even_slot, 4 - even_slot)
            allowed = band_ref[:, pl.ds(pl.multiple_of(slot * rows, rows), rows)] != 0
        if role == OWN:
            allowed = allowed | forced
        bias_ref[:, role * rows : (role + 1) * rows] = jnp.where(allowed, 0.0, -jnp.inf)

    place_in = quad_place[:, : QUAD * head]

    def own_lanes(stacked):
        picked = stacked[:rows]
        for member in range(1, QUAD):
            picked = jnp.where(
                place_in == member, stacked[member * rows : (member + 1) * rows], picked
            )
        return picked

    sinks = []
    for quad in range(HEADS // QUAD):
        for place in range(ROLES - 1):
            if quad == 0:
                arrival(place, 0).wait()
        cols = slice(quad * QUAD * head, (quad + 1) * QUAD * head)
        keys = jnp.concatenate(
            [own_ref[:rows, cols]] + [landed[place, :rows, cols] for place in range(ROLES - 1)], 0
        )
        vals = jnp.concatenate(
            [own_ref[rows:, cols]] + [landed[place, rows:, cols] for place in range(ROLES - 1)], 0
        )
        bias = bias_ref[...]
        scores = dot_nt(q2_ref[:, cols], keys) + jnp.concatenate([bias] * QUAD, 0)
        row_max = jnp.max(scores, axis=-1, keepdims=True)
        weights = jnp.exp(scores - row_max)
        row_total = jnp.sum(weights, axis=-1, keepdims=True)
        prob = weights * (1.0 / row_total)
        half = prob.astype(BF16)
        grad_prob = dot_nt(g2_ref[:, cols], vals)
        delta = jnp.sum(prob * grad_prob, axis=-1, keepdims=True)
        grad_score = (prob * (grad_prob - delta)).astype(BF16)
        att_ref[:, cols] = own_lanes(dot_nn(half, vals)).astype(BF16)
        dq_ref[:, cols] = (own_lanes(dot_nn(grad_score, keys)) * (1.0 / 8.0)).astype(BF16)
        copy = pltpu.make_async_copy(dq_ref.at[:, cols], dq_hbm.at[:, cols], sink_sems.at[quad])
        copy.start()
        sinks.append(copy)
        if quad == HEADS // QUAD - 1:
            out_ref[...] = dot_nn(att_ref[...], wo_ref[...]).astype(BF16)
            copy = pltpu.make_async_copy(out_ref, out_hbm, sink_sems.at[quad + 1])
            copy.start()
            sinks.append(copy)
        for member in range(QUAD // 2):
            start = (2 * quad + member) * pair
            span = slice(start, start + pair)
            mine = slice(member * 2 * rows, (member + 1) * 2 * rows)
            dkt = dot_nn(qt2_ref[span, :], grad_score[mine]).astype(BF16)
            dvt = dot_nn(gt2_ref[span, :], half[mine]).astype(BF16)
            for role, ref in enumerate(targets):
                ref[span, :] = dkt[:, role * rows : (role + 1) * rows]
                ref[width + start : width + start + pair, :] = dvt[
                    :, role * rows : (role + 1) * rows
                ]
    for copy in sinks:
        copy.wait()


def attend(side, q, g, wo, band, expander, own, remote):
    rows, width = q.shape
    return pl.pallas_call(
        heads_kernel,
        out_shape=[shape(rows, width)] * 2 + [shape(2 * width, rows)] * ROLES,
        in_specs=[SMEM] + [VMEM] * 6 + [HBM] * (ROLES - 1),
        out_specs=[HBM] * 2 + [VMEM] * ROLES,
        scratch_shapes=[
            pltpu.VMEM((rows, ROLES * rows), F32),
            pltpu.VMEM((QUAD * rows, width), BF16),
            pltpu.VMEM((QUAD * rows, width), BF16),
            pltpu.VMEM((width, 2 * rows), BF16),
            pltpu.VMEM((width, 2 * rows), BF16),
            pltpu.VMEM((rows, width), BF16),
            pltpu.VMEM((ROLES - 1, 2 * rows, width), BF16),
            pltpu.SemaphoreType.DMA((ROLES - 1, HEADS // QUAD)),
            pltpu.VMEM((rows, width), BF16),
            pltpu.VMEM((rows, width), BF16),
            pltpu.SemaphoreType.DMA((HEADS // QUAD + 1,)),
        ],
        compiler_params=LIMIT,
        name="heads",
    )(side, q, g, wo, band, expander, own, *remote)


def finish_kernel(wv_ref, own_ref, *refs):
    parts, (dk_hbm, df_hbm, dk_ref, df_ref, landed, sems) = refs[:-6], refs[-6:]
    width = wv_ref.shape[0]
    arrivals = [
        pltpu.make_async_copy(ref, landed.at[place], sems.at[place])
        for place, ref in enumerate(parts)
    ]
    for copy in arrivals:
        copy.start()
    for copy in arrivals:
        copy.wait()

    def total(span):
        summed = own_ref[span, :].astype(F32)
        for place in range(len(parts)):
            summed = summed + landed[place, span, :].astype(F32)
        return summed.T.astype(BF16)

    df_ref[...] = dot_nt(total(slice(width, 2 * width)), wv_ref[...]).astype(BF16)
    df_copy = pltpu.make_async_copy(df_ref, df_hbm, sems.at[len(parts) + 1])
    df_copy.start()
    dk_ref[...] = total(slice(0, width))
    dk_copy = pltpu.make_async_copy(dk_ref, dk_hbm, sems.at[len(parts)])
    dk_copy.start()
    dk_copy.wait()
    df_copy.wait()


def finish(wv, own, parts):
    rows = own.shape[1]
    width = wv.shape[0]
    return pl.pallas_call(
        finish_kernel,
        out_shape=[shape(rows, width)] * 2,
        in_specs=[VMEM] * 2 + [HBM] * len(parts),
        out_specs=[HBM] * 2,
        scratch_shapes=[
            pltpu.VMEM((rows, width), BF16),
            pltpu.VMEM((rows, width), BF16),
            pltpu.VMEM((len(parts), 2 * width, rows), BF16),
            pltpu.SemaphoreType.DMA((len(parts) + 2,)),
        ],
        compiler_params=LIMIT,
        name="finish",
    )(wv, own, *parts)


def send(value, route):
    count = lax.axis_size("blk")
    return lax.ppermute(value, "blk", [(s, route(s, count)) for s in range(count)])


def twin_of(s, count):
    return s ^ 1


def up_even(s, count):
    return (s + 2 - 4 * (s & 1)) % count


def down_even(s, count):
    return (s - 2 + 4 * (s & 1)) % count


def match_by(mask):
    return lambda s, count: s ^ mask


def gather(mask, key_vals, moved):
    inner = send(key_vals, down_even)
    match = send(moved, match_by(mask)) if mask else moved
    outer = send(key_vals, up_even)
    inner, key_vals = lax.optimization_barrier((inner, key_vals))
    twin = send(key_vals, twin_of)
    near = send(inner, twin_of)
    return outer, near, twin, inner, match


def scatter(mask, d_outer, d_near, d_twin, d_inner, d_match):
    joined = send(d_near, twin_of)
    match = send(d_match, match_by(mask)) if mask else d_match
    outer = send(d_outer, down_even)
    d_twin, joined = lax.optimization_barrier((d_twin, joined))
    twin = send(d_twin, twin_of)
    d_inner = (d_inner.astype(F32) + joined.astype(F32)).astype(BF16)
    inner = send(d_inner, up_even)
    return twin, outer, inner, match


def route_group(value, number, shift, size):
    def by(mask):
        return lambda moved: send(moved, match_by(mask << shift)) if mask else moved

    return lax.switch(number, [by(mask) for mask in range(size)], value)


def shards(
    queries, key_vectors, node_feats, w_value, w_out, band_mask, expander_mask, partner, out_grad
):
    count = lax.axis_size("blk")
    bits = count.bit_length() - 1
    place = lax.axis_index("blk")
    side = jnp.reshape(place & 1, (1,)).astype(jnp.int32)
    match_mask = jnp.bitwise_xor(partner[0], place)
    values = lax.dot_general(
        node_feats, w_value, (((1,), (0,)), ((), ())), preferred_element_type=F32
    ).astype(BF16)
    key_vals = jnp.concatenate([key_vectors, values], 0)
    first = min(bits, GROUP_BITS)
    groups = []
    for shift in range(first, bits, GROUP_BITS):
        width = min(GROUP_BITS, bits - shift)
        number = jnp.bitwise_and(jnp.right_shift(match_mask, shift), (1 << width) - 1)
        groups.append((number, shift, 1 << width))
    masks = range(0 if groups else 1, 1 << first)
    number = jnp.bitwise_and(match_mask, (1 << first) - 1) - masks[0]
    moved = key_vals
    for group in groups:
        moved = route_group(moved, *group)
    outer, near, twin, inner, match = lax.switch(
        number, [partial(gather, mask) for mask in masks], key_vals, moved
    )
    out, dq, d_own, d_outer, d_near, d_twin, d_inner, d_match = attend(
        side, queries, out_grad, w_out, band_mask, expander_mask,
        key_vals, (outer, near, twin, inner, match),
    )
    twin, outer, inner, match = lax.switch(
        number, [partial(scatter, mask) for mask in masks],
        d_outer, d_near, d_twin, d_inner, d_match,
    )
    for group in groups:
        match = route_group(match, *group)
    dk, df = finish(w_value, d_own, (twin, outer, inner, match))
    return out, dq, dk, df


def solution(mesh):
    split = P("blk", None)
    return jax.shard_map(
        shards,
        mesh=mesh,
        in_specs=(split, split, split, P(), P(), split, split, P("blk"), split),
        out_specs=(split, split, split, split),
        check_vma=False,
    )
```

```python
from functools import partial

import jax
import jax.numpy as jnp
from jax import lax
from jax.experimental import pallas as pl
from jax.experimental.pallas import tpu as pltpu
from jax.sharding import PartitionSpec as P

HEADS = 8
ROLES = 6
QUAD = 4
OWN, OUTER, NEAR, TWIN, INNER, MATCH = range(ROLES)
GROUP_BITS = 5
BF16 = jnp.bfloat16
F32 = jnp.float32
HBM = pl.BlockSpec(memory_space=pltpu.HBM)
VMEM = pl.BlockSpec(memory_space=pltpu.VMEM)
SMEM = pl.BlockSpec(memory_space=pltpu.SMEM)
LIMIT = pltpu.CompilerParams(vmem_limit_bytes=40 * 1024 * 1024)


def dot_nn(a, b):
    return lax.dot_general(a, b, (((1,), (0,)), ((), ())), preferred_element_type=F32)


def dot_nt(a, b):
    return lax.dot_general(a, b, (((1,), (1,)), ((), ())), preferred_element_type=F32)


def shape(*dims, kind=BF16):
    return jax.ShapeDtypeStruct(dims, kind)


def heads_kernel(*refs):
    side_ref, q_ref, g_ref, wo_ref, band_ref, exp_ref, own_ref = refs[:7]
    remote = refs[7 : 6 + ROLES]
    out_hbm, dq_hbm = refs[6 + ROLES : 8 + ROLES]
    targets = refs[8 + ROLES : 8 + 2 * ROLES]
    bias_ref, q2_ref, g2_ref, qt2_ref, gt2_ref, att_ref, landed, sems = refs[8 + 2 * ROLES : -3]
    out_ref, dq_ref, sink_sems = refs[-3:]
    rows, width = q_ref.shape
    head = width // HEADS
    pair = 2 * head

    def arrival(place, index):
        return pltpu.make_async_copy(remote[place], landed.at[place], sems.at[place, index])

    for place in range(ROLES - 1):
        arrival(place, 0).start()

    side = side_ref[0]
    lane = lax.broadcasted_iota(jnp.int32, (rows, width), 1)
    low = jnp.bitwise_and(lane, head) == 0
    quad_place = jnp.bitwise_and(lane, QUAD * head - 1) // head

    def spread(block, wide_ref, tall_ref):
        first = jnp.where(low, block, 0.0)
        second = jnp.where(low, 0.0, block)
        for member in range(QUAD):
            mine = quad_place == member
            wide_ref[member * rows : (member + 1) * rows, :] = jnp.where(mine, block, 0.0).astype(BF16)
        tall_ref[:, :rows] = first.T.astype(BF16)
        tall_ref[:, rows:] = second.T.astype(BF16)

    spread(q_ref[...].astype(F32) * (1.0 / 8.0), q2_ref, qt2_ref)
    grads = dot_nt(g_ref[...], wo_ref[...]).astype(BF16)
    spread(grads.astype(F32), g2_ref, gt2_ref)

    row_ids = lax.broadcasted_iota(jnp.int32, (rows, rows), 0)
    col_ids = lax.broadcasted_iota(jnp.int32, (rows, rows), 1)
    forced = (col_ids == row_ids) | (col_ids == jnp.bitwise_xor(row_ids, 1))
    for role, even_slot in ((OUTER, 0), (NEAR, 1), (OWN, 2), (TWIN, 3), (INNER, 4), (MATCH, None)):
        if role == MATCH:
            allowed = exp_ref[...] != 0
        else:
            slot = jnp.where(side == 0, even_slot, 4 - even_slot)
            allowed = band_ref[:, pl.ds(pl.multiple_of(slot * rows, rows), rows)] != 0
        if role == OWN:
            allowed = allowed | forced
        bias_ref[:, role * rows : (role + 1) * rows] = jnp.where(allowed, 0.0, -jnp.inf)

    place_in = quad_place[:, : QUAD * head]

    def own_lanes(stacked):
        picked = stacked[:rows]
        for member in range(1, QUAD):
            picked = jnp.where(
                place_in == member, stacked[member * rows : (member + 1) * rows], picked
            )
        return picked

    sinks = []
    for quad in range(HEADS // QUAD):
        for place in range(ROLES - 1):
            if quad == 0:
                arrival(place, 0).wait()
        cols = slice(quad * QUAD * head, (quad + 1) * QUAD * head)
        keys = jnp.concatenate(
            [own_ref[:rows, cols]] + [landed[place, :rows, cols] for place in range(ROLES - 1)], 0
        )
        vals = jnp.concatenate(
            [own_ref[rows:, cols]] + [landed[place, rows:, cols] for place in range(ROLES - 1)], 0
        )
        bias = bias_ref[...]
        scores = dot_nt(q2_ref[:, cols], keys) + jnp.concatenate([bias] * QUAD, 0)
        row_max = jnp.max(scores, axis=-1, keepdims=True)
        weights = jnp.exp(scores - row_max)
        row_total = jnp.sum(weights, axis=-1, keepdims=True)
        prob = weights * (1.0 / row_total)
        half = prob.astype(BF16)
        grad_prob = dot_nt(g2_ref[:, cols], vals)
        delta = jnp.sum(prob * grad_prob, axis=-1, keepdims=True)
        grad_score = (prob * (grad_prob - delta)).astype(BF16)
        att_ref[:, cols] = own_lanes(dot_nn(half, vals)).astype(BF16)
        dq_ref[:, cols] = (own_lanes(dot_nn(grad_score, keys)) * (1.0 / 8.0)).astype(BF16)
        copy = pltpu.make_async_copy(dq_ref.at[:, cols], dq_hbm.at[:, cols], sink_sems.at[quad])
        copy.start()
        sinks.append(copy)
        if quad == HEADS // QUAD - 1:
            out_ref[...] = dot_nn(att_ref[...], wo_ref[...]).astype(BF16)
            copy = pltpu.make_async_copy(out_ref, out_hbm, sink_sems.at[quad + 1])
            copy.start()
            sinks.append(copy)
        for member in range(QUAD // 2):
            start = (2 * quad + member) * pair
            span = slice(start, start + pair)
            mine = slice(member * 2 * rows, (member + 1) * 2 * rows)
            dkt = dot_nn(qt2_ref[span, :], grad_score[mine]).astype(BF16)
            dvt = dot_nn(gt2_ref[span, :], half[mine]).astype(BF16)
            for role, ref in enumerate(targets):
                ref[span, :] = dkt[:, role * rows : (role + 1) * rows]
                ref[width + start : width + start + pair, :] = dvt[
                    :, role * rows : (role + 1) * rows
                ]
    for copy in sinks:
        copy.wait()


def attend(side, q, g, wo, band, expander, own, remote):
    rows, width = q.shape
    return pl.pallas_call(
        heads_kernel,
        out_shape=[shape(rows, width)] * 2 + [shape(2 * width, rows)] * ROLES,
        in_specs=[SMEM] + [VMEM] * 6 + [HBM] * (ROLES - 1),
        out_specs=[HBM] * 2 + [VMEM] * ROLES,
        scratch_shapes=[
            pltpu.VMEM((rows, ROLES * rows), F32),
            pltpu.VMEM((QUAD * rows, width), BF16),
            pltpu.VMEM((QUAD * rows, width), BF16),
            pltpu.VMEM((width, 2 * rows), BF16),
            pltpu.VMEM((width, 2 * rows), BF16),
            pltpu.VMEM((rows, width), BF16),
            pltpu.VMEM((ROLES - 1, 2 * rows, width), BF16),
            pltpu.SemaphoreType.DMA((ROLES - 1, HEADS // QUAD)),
            pltpu.VMEM((rows, width), BF16),
            pltpu.VMEM((rows, width), BF16),
            pltpu.SemaphoreType.DMA((HEADS // QUAD + 1,)),
        ],
        compiler_params=LIMIT,
        name="heads",
    )(side, q, g, wo, band, expander, own, *remote)


def finish_kernel(wv_ref, own_ref, *refs):
    parts, (dk_hbm, df_hbm, dk_ref, df_ref, landed, sems) = refs[:-6], refs[-6:]
    width = wv_ref.shape[0]
    arrivals = [
        pltpu.make_async_copy(ref, landed.at[place], sems.at[place])
        for place, ref in enumerate(parts)
    ]
    for copy in arrivals:
        copy.start()
    for copy in arrivals:
        copy.wait()

    def total(span):
        summed = own_ref[span, :].astype(F32)
        for place in range(len(parts)):
            summed = summed + landed[place, span, :].astype(F32)
        return summed.T.astype(BF16)

    df_ref[...] = dot_nt(total(slice(width, 2 * width)), wv_ref[...]).astype(BF16)
    df_copy = pltpu.make_async_copy(df_ref, df_hbm, sems.at[len(parts) + 1])
    df_copy.start()
    dk_ref[...] = total(slice(0, width))
    dk_copy = pltpu.make_async_copy(dk_ref, dk_hbm, sems.at[len(parts)])
    dk_copy.start()
    dk_copy.wait()
    df_copy.wait()


def finish(wv, own, parts):
    rows = own.shape[1]
    width = wv.shape[0]
    return pl.pallas_call(
        finish_kernel,
        out_shape=[shape(rows, width)] * 2,
        in_specs=[VMEM] * 2 + [HBM] * len(parts),
        out_specs=[HBM] * 2,
        scratch_shapes=[
            pltpu.VMEM((rows, width), BF16),
            pltpu.VMEM((rows, width), BF16),
            pltpu.VMEM((len(parts), 2 * width, rows), BF16),
            pltpu.SemaphoreType.DMA((len(parts) + 2,)),
        ],
        compiler_params=LIMIT,
        name="finish",
    )(wv, own, *parts)


def send(value, route):
    count = lax.axis_size("blk")
    return lax.ppermute(value, "blk", [(s, route(s, count)) for s in range(count)])


def twin_of(s, count):
    return s ^ 1


def up_even(s, count):
    return (s + 2 - 4 * (s & 1)) % count


def down_even(s, count):
    return (s - 2 + 4 * (s & 1)) % count


def match_by(mask):
    return lambda s, count: s ^ mask


GATHER_ORDER = {16: 'match later', 21: 'match later', 25: 'match later'}
SCATTER_ORDER = {8: 'match first', 16: 'match first', 17: 'match first', 20: 'match first', 21: 'match first', 23: 'match first', 9: 'match later', 10: 'match later', 15: 'match later'}


def order_of(table, mask):
    return table.get(mask, "") if lax.axis_size("blk") == 32 else ""


def gather(mask, key_vals, moved):
    order = order_of(GATHER_ORDER, mask)
    if order:
        twin = send(key_vals, twin_of)
        twin, moved = lax.optimization_barrier((twin, moved))
    inner = send(key_vals, down_even)
    match = send(moved, match_by(mask)) if mask else moved
    outer = send(key_vals, up_even)
    if not order:
        inner, key_vals = lax.optimization_barrier((inner, key_vals))
        twin = send(key_vals, twin_of)
    near = send(inner, twin_of)
    return outer, near, twin, inner, match


def scatter(mask, d_outer, d_near, d_twin, d_inner, d_match):
    order = order_of(SCATTER_ORDER, mask)
    joined = send(d_near, twin_of)
    if order == "match first":
        d_outer, joined = lax.optimization_barrier((d_outer, joined))
    elif order == "match later":
        d_match, joined = lax.optimization_barrier((d_match, joined))
    match = send(d_match, match_by(mask)) if mask else d_match
    outer = send(d_outer, down_even)
    d_twin, joined = lax.optimization_barrier((d_twin, joined))
    twin = send(d_twin, twin_of)
    d_inner = (d_inner.astype(F32) + joined.astype(F32)).astype(BF16)
    inner = send(d_inner, up_even)
    return twin, outer, inner, match


def route_group(value, number, shift, size):
    def by(mask):
        return lambda moved: send(moved, match_by(mask << shift)) if mask else moved

    return lax.switch(number, [by(mask) for mask in range(size)], value)


def shards(
    queries, key_vectors, node_feats, w_value, w_out, band_mask, expander_mask, partner, out_grad
):
    count = lax.axis_size("blk")
    bits = count.bit_length() - 1
    place = lax.axis_index("blk")
    side = jnp.reshape(place & 1, (1,)).astype(jnp.int32)
    match_mask = jnp.bitwise_xor(partner[0], place)
    values = lax.dot_general(
        node_feats, w_value, (((1,), (0,)), ((), ())), preferred_element_type=F32
    ).astype(BF16)
    key_vals = jnp.concatenate([key_vectors, values], 0)
    first = min(bits, GROUP_BITS)
    groups = []
    for shift in range(first, bits, GROUP_BITS):
        width = min(GROUP_BITS, bits - shift)
        number = jnp.bitwise_and(jnp.right_shift(match_mask, shift), (1 << width) - 1)
        groups.append((number, shift, 1 << width))
    masks = range(0 if groups else 1, 1 << first)
    number = jnp.bitwise_and(match_mask, (1 << first) - 1) - masks[0]
    moved = key_vals
    for group in groups:
        moved = route_group(moved, *group)
    outer, near, twin, inner, match = lax.switch(
        number, [partial(gather, mask) for mask in masks], key_vals, moved
    )
    out, dq, d_own, d_outer, d_near, d_twin, d_inner, d_match = attend(
        side, queries, out_grad, w_out, band_mask, expander_mask,
        key_vals, (outer, near, twin, inner, match),
    )
    twin, outer, inner, match = lax.switch(
        number, [partial(scatter, mask) for mask in masks],
        d_outer, d_near, d_twin, d_inner, d_match,
    )
    for group in groups:
        match = route_group(match, *group)
    dk, df = finish(w_value, d_own, (twin, outer, inner, match))
    return out, dq, dk, df


def solution(mesh):
    split = P("blk", None)
    return jax.shard_map(
        shards,
        mesh=mesh,
        in_specs=(split, split, split, P(), P(), split, split, P("blk"), split),
        out_specs=(split, split, split, split),
        check_vma=False,
    )
```

```python
from functools import partial

import jax
import jax.numpy as jnp
from jax import lax
from jax.experimental import pallas as pl
from jax.experimental.pallas import tpu as pltpu
from jax.sharding import PartitionSpec as P

HEADS = 8
ROLES = 6
QUAD = 4
OWN, OUTER, NEAR, TWIN, INNER, MATCH = range(ROLES)
GROUP_BITS = 5
BF16 = jnp.bfloat16
F32 = jnp.float32
HBM = pl.BlockSpec(memory_space=pltpu.HBM)
VMEM = pl.BlockSpec(memory_space=pltpu.VMEM)
SMEM = pl.BlockSpec(memory_space=pltpu.SMEM)
LIMIT = pltpu.CompilerParams(vmem_limit_bytes=40 * 1024 * 1024)


def dot_nn(a, b):
    return lax.dot_general(a, b, (((1,), (0,)), ((), ())), preferred_element_type=F32)


def dot_nt(a, b):
    return lax.dot_general(a, b, (((1,), (1,)), ((), ())), preferred_element_type=F32)


def shape(*dims, kind=BF16):
    return jax.ShapeDtypeStruct(dims, kind)


def heads_kernel(*refs):
    side_ref, q_ref, g_ref, wo_ref, band_ref, exp_ref, own_ref = refs[:7]
    remote = refs[7 : 6 + ROLES]
    out_hbm, dq_hbm = refs[6 + ROLES : 8 + ROLES]
    targets = refs[8 + ROLES : 8 + 2 * ROLES]
    bias_ref, q2_ref, g2_ref, qt2_ref, gt2_ref, att_ref, landed, sems = refs[8 + 2 * ROLES : -3]
    out_ref, dq_ref, sink_sems = refs[-3:]
    rows, width = q_ref.shape
    head = width // HEADS
    pair = 2 * head

    def arrival(place, index):
        return pltpu.make_async_copy(remote[place], landed.at[place], sems.at[place, index])

    for place in range(ROLES - 1):
        arrival(place, 0).start()

    side = side_ref[0]
    lane = lax.broadcasted_iota(jnp.int32, (rows, width), 1)
    low = jnp.bitwise_and(lane, head) == 0
    quad_place = jnp.bitwise_and(lane, QUAD * head - 1) // head

    def spread(block, wide_ref, tall_ref):
        first = jnp.where(low, block, 0.0)
        second = jnp.where(low, 0.0, block)
        for member in range(QUAD):
            mine = quad_place == member
            wide_ref[member * rows : (member + 1) * rows, :] = jnp.where(mine, block, 0.0).astype(BF16)
        tall_ref[:, :rows] = first.T.astype(BF16)
        tall_ref[:, rows:] = second.T.astype(BF16)

    spread(q_ref[...].astype(F32) * (1.0 / 8.0), q2_ref, qt2_ref)
    grads = dot_nt(g_ref[...], wo_ref[...]).astype(BF16)
    spread(grads.astype(F32), g2_ref, gt2_ref)

    row_ids = lax.broadcasted_iota(jnp.int32, (rows, rows), 0)
    col_ids = lax.broadcasted_iota(jnp.int32, (rows, rows), 1)
    forced = (col_ids == row_ids) | (col_ids == jnp.bitwise_xor(row_ids, 1))
    for role, even_slot in ((OUTER, 0), (NEAR, 1), (OWN, 2), (TWIN, 3), (INNER, 4), (MATCH, None)):
        if role == MATCH:
            allowed = exp_ref[...] != 0
        else:
            slot = jnp.where(side == 0, even_slot, 4 - even_slot)
            allowed = band_ref[:, pl.ds(pl.multiple_of(slot * rows, rows), rows)] != 0
        if role == OWN:
            allowed = allowed | forced
        bias_ref[:, role * rows : (role + 1) * rows] = jnp.where(allowed, 0.0, -jnp.inf)

    place_in = quad_place[:, : QUAD * head]

    def own_lanes(stacked):
        picked = stacked[:rows]
        for member in range(1, QUAD):
            picked = jnp.where(
                place_in == member, stacked[member * rows : (member + 1) * rows], picked
            )
        return picked

    sinks = []
    for quad in range(HEADS // QUAD):
        for place in range(ROLES - 1):
            if quad == 0:
                arrival(place, 0).wait()
        cols = slice(quad * QUAD * head, (quad + 1) * QUAD * head)
        keys = jnp.concatenate(
            [own_ref[:rows, cols]] + [landed[place, :rows, cols] for place in range(ROLES - 1)], 0
        )
        vals = jnp.concatenate(
            [own_ref[rows:, cols]] + [landed[place, rows:, cols] for place in range(ROLES - 1)], 0
        )
        bias = bias_ref[...]
        scores = dot_nt(q2_ref[:, cols], keys) + jnp.concatenate([bias] * QUAD, 0)
        row_max = jnp.max(scores, axis=-1, keepdims=True)
        weights = jnp.exp(scores - row_max)
        row_total = jnp.sum(weights, axis=-1, keepdims=True)
        prob = weights * (1.0 / row_total)
        half = prob.astype(BF16)
        grad_prob = dot_nt(g2_ref[:, cols], vals)
        delta = jnp.sum(prob * grad_prob, axis=-1, keepdims=True)
        grad_score = (prob * (grad_prob - delta)).astype(BF16)
        att_ref[:, cols] = own_lanes(dot_nn(half, vals)).astype(BF16)
        dq_ref[:, cols] = (own_lanes(dot_nn(grad_score, keys)) * (1.0 / 8.0)).astype(BF16)
        copy = pltpu.make_async_copy(dq_ref.at[:, cols], dq_hbm.at[:, cols], sink_sems.at[quad])
        copy.start()
        sinks.append(copy)
        if quad == HEADS // QUAD - 1:
            out_ref[...] = dot_nn(att_ref[...], wo_ref[...]).astype(BF16)
            copy = pltpu.make_async_copy(out_ref, out_hbm, sink_sems.at[quad + 1])
            copy.start()
            sinks.append(copy)
        for member in range(QUAD // 2):
            start = (2 * quad + member) * pair
            span = slice(start, start + pair)
            mine = slice(member * 2 * rows, (member + 1) * 2 * rows)
            dkt = dot_nn(qt2_ref[span, :], grad_score[mine]).astype(BF16)
            dvt = dot_nn(gt2_ref[span, :], half[mine]).astype(BF16)
            for role, ref in enumerate(targets):
                ref[span, :] = dkt[:, role * rows : (role + 1) * rows]
                ref[width + start : width + start + pair, :] = dvt[
                    :, role * rows : (role + 1) * rows
                ]
    for copy in sinks:
        copy.wait()


def attend(side, q, g, wo, band, expander, own, remote):
    rows, width = q.shape
    return pl.pallas_call(
        heads_kernel,
        out_shape=[shape(rows, width)] * 2 + [shape(2 * width, rows)] * ROLES,
        in_specs=[SMEM] + [VMEM] * 6 + [HBM] * (ROLES - 1),
        out_specs=[HBM] * 2 + [VMEM] * ROLES,
        scratch_shapes=[
            pltpu.VMEM((rows, ROLES * rows), F32),
            pltpu.VMEM((QUAD * rows, width), BF16),
            pltpu.VMEM((QUAD * rows, width), BF16),
            pltpu.VMEM((width, 2 * rows), BF16),
            pltpu.VMEM((width, 2 * rows), BF16),
            pltpu.VMEM((rows, width), BF16),
            pltpu.VMEM((ROLES - 1, 2 * rows, width), BF16),
            pltpu.SemaphoreType.DMA((ROLES - 1, HEADS // QUAD)),
            pltpu.VMEM((rows, width), BF16),
            pltpu.VMEM((rows, width), BF16),
            pltpu.SemaphoreType.DMA((HEADS // QUAD + 1,)),
        ],
        compiler_params=LIMIT,
        name="heads",
    )(side, q, g, wo, band, expander, own, *remote)


def finish_kernel(wv_ref, own_ref, *refs):
    parts, (dk_hbm, df_hbm, dk_ref, df_ref, landed, sems) = refs[:-6], refs[-6:]
    width = wv_ref.shape[0]
    arrivals = [
        pltpu.make_async_copy(ref, landed.at[place], sems.at[place])
        for place, ref in enumerate(parts)
    ]
    for copy in arrivals:
        copy.start()
    for copy in arrivals:
        copy.wait()

    def total(span):
        summed = own_ref[span, :].astype(F32)
        for place in range(len(parts)):
            summed = summed + landed[place, span, :].astype(F32)
        return summed.T.astype(BF16)

    df_ref[...] = dot_nt(total(slice(width, 2 * width)), wv_ref[...]).astype(BF16)
    df_copy = pltpu.make_async_copy(df_ref, df_hbm, sems.at[len(parts) + 1])
    df_copy.start()
    dk_ref[...] = total(slice(0, width))
    dk_copy = pltpu.make_async_copy(dk_ref, dk_hbm, sems.at[len(parts)])
    dk_copy.start()
    dk_copy.wait()
    df_copy.wait()


def finish(wv, own, parts):
    rows = own.shape[1]
    width = wv.shape[0]
    return pl.pallas_call(
        finish_kernel,
        out_shape=[shape(rows, width)] * 2,
        in_specs=[VMEM] * 2 + [HBM] * len(parts),
        out_specs=[HBM] * 2,
        scratch_shapes=[
            pltpu.VMEM((rows, width), BF16),
            pltpu.VMEM((rows, width), BF16),
            pltpu.VMEM((len(parts), 2 * width, rows), BF16),
            pltpu.SemaphoreType.DMA((len(parts) + 2,)),
        ],
        compiler_params=LIMIT,
        name="finish",
    )(wv, own, *parts)


def send(value, route):
    count = lax.axis_size("blk")
    return lax.ppermute(value, "blk", [(s, route(s, count)) for s in range(count)])


def twin_of(s, count):
    return s ^ 1


def up_even(s, count):
    return (s + 2 - 4 * (s & 1)) % count


def down_even(s, count):
    return (s - 2 + 4 * (s & 1)) % count


def match_by(mask):
    return lambda s, count: s ^ mask


GATHER_ORDER = {16: 'match later', 21: 'match later', 25: 'match later'}
SCATTER_ORDER = {8: 'match first', 16: 'match first', 17: 'match first', 20: 'match first', 21: 'match first', 23: 'match first', 9: 'match later', 10: 'match later', 15: 'match later'}


def order_of(table, mask):
    return table.get(mask, "") if lax.axis_size("blk") == 32 else ""


def is_beside(mask):
    return mask == 2 and lax.axis_size("blk") <= 1 << GROUP_BITS


def beside_is_inner():
    place = lax.axis_index("blk")
    return jnp.bitwise_and(jnp.bitwise_xor(place, jnp.right_shift(place, 1)), 1) == 0


def gather(mask, key_vals, moved):
    order = order_of(GATHER_ORDER, mask)
    if order:
        twin = send(key_vals, twin_of)
        twin, moved = lax.optimization_barrier((twin, moved))
    inner = send(key_vals, down_even)
    outer = send(key_vals, up_even)
    if is_beside(mask):
        match = jnp.where(beside_is_inner(), inner, outer)
    else:
        match = send(moved, match_by(mask)) if mask else moved
    if not order:
        inner, key_vals = lax.optimization_barrier((inner, key_vals))
        twin = send(key_vals, twin_of)
    near = send(inner, twin_of)
    return outer, near, twin, inner, match


def scatter(mask, d_outer, d_near, d_twin, d_inner, d_match):
    order = order_of(SCATTER_ORDER, mask)
    joined = send(d_near, twin_of)
    if order == "match first":
        d_outer, joined = lax.optimization_barrier((d_outer, joined))
    elif order == "match later":
        d_match, joined = lax.optimization_barrier((d_match, joined))
    if is_beside(mask):
        match = jnp.zeros_like(d_match)
        d_match = d_match.astype(F32)
        to_inner = jnp.where(beside_is_inner(), d_match, 0.0)
        to_outer = jnp.where(beside_is_inner(), 0.0, d_match)
        d_outer = (d_outer.astype(F32) + to_outer).astype(BF16)
    else:
        match = send(d_match, match_by(mask)) if mask else d_match
    outer = send(d_outer, down_even)
    d_twin, joined = lax.optimization_barrier((d_twin, joined))
    twin = send(d_twin, twin_of)
    d_inner = d_inner.astype(F32) + joined.astype(F32)
    if is_beside(mask):
        d_inner = d_inner + to_inner
    d_inner = d_inner.astype(BF16)
    inner = send(d_inner, up_even)
    return twin, outer, inner, match


def route_group(value, number, shift, size):
    def by(mask):
        return lambda moved: send(moved, match_by(mask << shift)) if mask else moved

    return lax.switch(number, [by(mask) for mask in range(size)], value)


def shards(
    queries, key_vectors, node_feats, w_value, w_out, band_mask, expander_mask, partner, out_grad
):
    count = lax.axis_size("blk")
    bits = count.bit_length() - 1
    place = lax.axis_index("blk")
    side = jnp.reshape(place & 1, (1,)).astype(jnp.int32)
    match_mask = jnp.bitwise_xor(partner[0], place)
    values = lax.dot_general(
        node_feats, w_value, (((1,), (0,)), ((), ())), preferred_element_type=F32
    ).astype(BF16)
    key_vals = jnp.concatenate([key_vectors, values], 0)
    first = min(bits, GROUP_BITS)
    groups = []
    for shift in range(first, bits, GROUP_BITS):
        width = min(GROUP_BITS, bits - shift)
        number = jnp.bitwise_and(jnp.right_shift(match_mask, shift), (1 << width) - 1)
        groups.append((number, shift, 1 << width))
    masks = range(0 if groups else 1, 1 << first)
    number = jnp.bitwise_and(match_mask, (1 << first) - 1) - masks[0]
    moved = key_vals
    for group in groups:
        moved = route_group(moved, *group)
    outer, near, twin, inner, match = lax.switch(
        number, [partial(gather, mask) for mask in masks], key_vals, moved
    )
    out, dq, d_own, d_outer, d_near, d_twin, d_inner, d_match = attend(
        side, queries, out_grad, w_out, band_mask, expander_mask,
        key_vals, (outer, near, twin, inner, match),
    )
    twin, outer, inner, match = lax.switch(
        number, [partial(scatter, mask) for mask in masks],
        d_outer, d_near, d_twin, d_inner, d_match,
    )
    for group in groups:
        match = route_group(match, *group)
    dk, df = finish(w_value, d_own, (twin, outer, inner, match))
    return out, dq, dk, df


def solution(mesh):
    split = P("blk", None)
    return jax.shard_map(
        shards,
        mesh=mesh,
        in_specs=(split, split, split, P(), P(), split, split, P("blk"), split),
        out_specs=(split, split, split, split),
        check_vma=False,
    )
```

```python
from functools import partial

import jax
import jax.numpy as jnp
from jax import lax
from jax.experimental import pallas as pl
from jax.experimental.pallas import tpu as pltpu
from jax.sharding import PartitionSpec as P

HEADS = 8
ROLES = 6
QUAD = 4
OWN, OUTER, NEAR, TWIN, INNER, MATCH = range(ROLES)
GROUP_BITS = 5
BF16 = jnp.bfloat16
F32 = jnp.float32
HBM = pl.BlockSpec(memory_space=pltpu.HBM)
VMEM = pl.BlockSpec(memory_space=pltpu.VMEM)
SMEM = pl.BlockSpec(memory_space=pltpu.SMEM)
LIMIT = pltpu.CompilerParams(vmem_limit_bytes=40 * 1024 * 1024)


def dot_nn(a, b):
    return lax.dot_general(a, b, (((1,), (0,)), ((), ())), preferred_element_type=F32)


def dot_nt(a, b):
    return lax.dot_general(a, b, (((1,), (1,)), ((), ())), preferred_element_type=F32)


def shape(*dims, kind=BF16):
    return jax.ShapeDtypeStruct(dims, kind)


def heads_kernel(*refs):
    side_ref, q_ref, g_ref, wo_ref, band_ref, exp_ref, own_ref = refs[:7]
    remote = refs[7 : 6 + ROLES]
    out_hbm, dq_hbm = refs[6 + ROLES : 8 + ROLES]
    targets = refs[8 + ROLES : 8 + 2 * ROLES]
    bias_ref, q2_ref, g2_ref, qt2_ref, gt2_ref, att_ref, landed, sems = refs[8 + 2 * ROLES : -3]
    out_ref, dq_ref, sink_sems = refs[-3:]
    rows, width = q_ref.shape
    head = width // HEADS
    pair = 2 * head

    def arrival(place, index):
        return pltpu.make_async_copy(remote[place], landed.at[place], sems.at[place, index])

    for place in range(ROLES - 1):
        arrival(place, 0).start()

    side = side_ref[0]
    lane = lax.broadcasted_iota(jnp.int32, (rows, width), 1)
    low = jnp.bitwise_and(lane, head) == 0
    quad_place = jnp.bitwise_and(lane, QUAD * head - 1) // head

    def spread(block, wide_ref, tall_ref):
        first = jnp.where(low, block, 0.0)
        second = jnp.where(low, 0.0, block)
        for member in range(QUAD):
            mine = quad_place == member
            wide_ref[member * rows : (member + 1) * rows, :] = jnp.where(mine, block, 0.0).astype(BF16)
        tall_ref[:, :rows] = first.T.astype(BF16)
        tall_ref[:, rows:] = second.T.astype(BF16)

    spread(q_ref[...].astype(F32) * (1.0 / 8.0), q2_ref, qt2_ref)
    grads = dot_nt(g_ref[...], wo_ref[...]).astype(BF16)
    spread(grads.astype(F32), g2_ref, gt2_ref)

    row_ids = lax.broadcasted_iota(jnp.int32, (rows, rows), 0)
    col_ids = lax.broadcasted_iota(jnp.int32, (rows, rows), 1)
    forced = (col_ids == row_ids) | (col_ids == jnp.bitwise_xor(row_ids, 1))
    for role, even_slot in ((OUTER, 0), (NEAR, 1), (OWN, 2), (TWIN, 3), (INNER, 4), (MATCH, None)):
        if role == MATCH:
            allowed = exp_ref[...] != 0
        else:
            slot = jnp.where(side == 0, even_slot, 4 - even_slot)
            allowed = band_ref[:, pl.ds(pl.multiple_of(slot * rows, rows), rows)] != 0
        if role == OWN:
            allowed = allowed | forced
        bias_ref[:, role * rows : (role + 1) * rows] = jnp.where(allowed, 0.0, -jnp.inf)

    place_in = quad_place[:, : QUAD * head]

    def own_lanes(stacked):
        picked = stacked[:rows]
        for member in range(1, QUAD):
            picked = jnp.where(
                place_in == member, stacked[member * rows : (member + 1) * rows], picked
            )
        return picked

    sinks = []
    for quad in range(HEADS // QUAD):
        for place in range(ROLES - 1):
            if quad == 0:
                arrival(place, 0).wait()
        cols = slice(quad * QUAD * head, (quad + 1) * QUAD * head)
        keys = jnp.concatenate(
            [own_ref[:rows, cols]] + [landed[place, :rows, cols] for place in range(ROLES - 1)], 0
        )
        vals = jnp.concatenate(
            [own_ref[rows:, cols]] + [landed[place, rows:, cols] for place in range(ROLES - 1)], 0
        )
        bias = bias_ref[...]
        scores = dot_nt(q2_ref[:, cols], keys) + jnp.concatenate([bias] * QUAD, 0)
        row_max = jnp.max(scores, axis=-1, keepdims=True)
        weights = jnp.exp(scores - row_max)
        row_total = jnp.sum(weights, axis=-1, keepdims=True)
        prob = weights * (1.0 / row_total)
        half = prob.astype(BF16)
        grad_prob = dot_nt(g2_ref[:, cols], vals)
        delta = jnp.sum(prob * grad_prob, axis=-1, keepdims=True)
        grad_score = (prob * (grad_prob - delta)).astype(BF16)
        att_ref[:, cols] = own_lanes(dot_nn(half, vals)).astype(BF16)
        dq_ref[:, cols] = (own_lanes(dot_nn(grad_score, keys)) * (1.0 / 8.0)).astype(BF16)
        copy = pltpu.make_async_copy(dq_ref.at[:, cols], dq_hbm.at[:, cols], sink_sems.at[quad])
        copy.start()
        sinks.append(copy)
        if quad == HEADS // QUAD - 1:
            out_ref[...] = dot_nn(att_ref[...], wo_ref[...]).astype(BF16)
            copy = pltpu.make_async_copy(out_ref, out_hbm, sink_sems.at[quad + 1])
            copy.start()
            sinks.append(copy)
        for member in range(QUAD // 2):
            start = (2 * quad + member) * pair
            span = slice(start, start + pair)
            mine = slice(member * 2 * rows, (member + 1) * 2 * rows)
            dkt = dot_nn(qt2_ref[span, :], grad_score[mine]).astype(BF16)
            dvt = dot_nn(gt2_ref[span, :], half[mine]).astype(BF16)
            for role, ref in enumerate(targets):
                ref[span, :] = dkt[:, role * rows : (role + 1) * rows]
                ref[width + start : width + start + pair, :] = dvt[
                    :, role * rows : (role + 1) * rows
                ]
    for copy in sinks:
        copy.wait()


def attend(side, q, g, wo, band, expander, own, remote):
    rows, width = q.shape
    return pl.pallas_call(
        heads_kernel,
        out_shape=[shape(rows, width)] * 2 + [shape(2 * width, rows)] * ROLES,
        in_specs=[SMEM] + [VMEM] * 6 + [HBM] * (ROLES - 1),
        out_specs=[HBM] * 2 + [VMEM] * ROLES,
        scratch_shapes=[
            pltpu.VMEM((rows, ROLES * rows), F32),
            pltpu.VMEM((QUAD * rows, width), BF16),
            pltpu.VMEM((QUAD * rows, width), BF16),
            pltpu.VMEM((width, 2 * rows), BF16),
            pltpu.VMEM((width, 2 * rows), BF16),
            pltpu.VMEM((rows, width), BF16),
            pltpu.VMEM((ROLES - 1, 2 * rows, width), BF16),
            pltpu.SemaphoreType.DMA((ROLES - 1, HEADS // QUAD)),
            pltpu.VMEM((rows, width), BF16),
            pltpu.VMEM((rows, width), BF16),
            pltpu.SemaphoreType.DMA((HEADS // QUAD + 1,)),
        ],
        compiler_params=LIMIT,
        name="heads",
    )(side, q, g, wo, band, expander, own, *remote)


def finish_kernel(wv_ref, own_ref, *refs):
    parts, (dk_hbm, df_hbm, dk_ref, df_ref, landed, sems) = refs[:-6], refs[-6:]
    width = wv_ref.shape[0]
    arrivals = [
        pltpu.make_async_copy(ref, landed.at[place], sems.at[place])
        for place, ref in enumerate(parts)
    ]
    for copy in arrivals:
        copy.start()
    for copy in arrivals:
        copy.wait()

    def total(span):
        summed = own_ref[span, :].astype(F32)
        for place in range(len(parts)):
            summed = summed + landed[place, span, :].astype(F32)
        return summed.T.astype(BF16)

    df_ref[...] = dot_nt(total(slice(width, 2 * width)), wv_ref[...]).astype(BF16)
    df_copy = pltpu.make_async_copy(df_ref, df_hbm, sems.at[len(parts) + 1])
    df_copy.start()
    dk_ref[...] = total(slice(0, width))
    dk_copy = pltpu.make_async_copy(dk_ref, dk_hbm, sems.at[len(parts)])
    dk_copy.start()
    dk_copy.wait()
    df_copy.wait()


def finish(wv, own, parts):
    rows = own.shape[1]
    width = wv.shape[0]
    return pl.pallas_call(
        finish_kernel,
        out_shape=[shape(rows, width)] * 2,
        in_specs=[VMEM] * 2 + [HBM] * len(parts),
        out_specs=[HBM] * 2,
        scratch_shapes=[
            pltpu.VMEM((rows, width), BF16),
            pltpu.VMEM((rows, width), BF16),
            pltpu.VMEM((len(parts), 2 * width, rows), BF16),
            pltpu.SemaphoreType.DMA((len(parts) + 2,)),
        ],
        compiler_params=LIMIT,
        name="finish",
    )(wv, own, *parts)


def send(value, route):
    count = lax.axis_size("blk")
    return lax.ppermute(value, "blk", [(s, route(s, count)) for s in range(count)])


def twin_of(s, count):
    return s ^ 1


def up_even(s, count):
    return (s + 2 - 4 * (s & 1)) % count


def down_even(s, count):
    return (s - 2 + 4 * (s & 1)) % count


def match_by(mask):
    return lambda s, count: s ^ mask


GATHER_ORDER = {16: 'match later', 25: 'match later'}
SCATTER_ORDER = {8: 'match first', 16: 'match first', 17: 'match first', 20: 'match first', 21: 'match first', 23: 'match first', 9: 'match later', 10: 'match later', 15: 'match later'}


def order_of(table, mask):
    return table.get(mask, "") if lax.axis_size("blk") == 32 else ""


def is_beside(mask):
    return mask == 2 and lax.axis_size("blk") <= 1 << GROUP_BITS


def beside_is_inner():
    place = lax.axis_index("blk")
    return jnp.bitwise_and(jnp.bitwise_xor(place, jnp.right_shift(place, 1)), 1) == 0


def gather(mask, key_vals, moved):
    order = order_of(GATHER_ORDER, mask)
    if order:
        twin = send(key_vals, twin_of)
        twin, moved = lax.optimization_barrier((twin, moved))
    inner = send(key_vals, down_even)
    outer = send(key_vals, up_even)
    if is_beside(mask):
        match = jnp.where(beside_is_inner(), inner, outer)
    else:
        match = send(moved, match_by(mask)) if mask else moved
    if not order:
        inner, key_vals = lax.optimization_barrier((inner, key_vals))
        twin = send(key_vals, twin_of)
    near = send(inner, twin_of)
    return outer, near, twin, inner, match


def scatter(mask, d_outer, d_near, d_twin, d_inner, d_match):
    order = order_of(SCATTER_ORDER, mask)
    joined = send(d_near, twin_of)
    if order == "match first":
        d_outer, joined = lax.optimization_barrier((d_outer, joined))
    elif order == "match later":
        d_match, joined = lax.optimization_barrier((d_match, joined))
    if is_beside(mask):
        match = jnp.zeros_like(d_match)
        d_match = d_match.astype(F32)
        to_inner = jnp.where(beside_is_inner(), d_match, 0.0)
        to_outer = jnp.where(beside_is_inner(), 0.0, d_match)
        d_outer = (d_outer.astype(F32) + to_outer).astype(BF16)
    else:
        match = send(d_match, match_by(mask)) if mask else d_match
    outer = send(d_outer, down_even)
    d_twin, joined = lax.optimization_barrier((d_twin, joined))
    twin = send(d_twin, twin_of)
    d_inner = d_inner.astype(F32) + joined.astype(F32)
    if is_beside(mask):
        d_inner = d_inner + to_inner
    d_inner = d_inner.astype(BF16)
    inner = send(d_inner, up_even)
    return twin, outer, inner, match


def route_group(value, number, shift, size):
    def by(mask):
        return lambda moved: send(moved, match_by(mask << shift)) if mask else moved

    return lax.switch(number, [by(mask) for mask in range(size)], value)


def shards(
    queries, key_vectors, node_feats, w_value, w_out, band_mask, expander_mask, partner, out_grad
):
    count = lax.axis_size("blk")
    bits = count.bit_length() - 1
    place = lax.axis_index("blk")
    side = jnp.reshape(place & 1, (1,)).astype(jnp.int32)
    match_mask = jnp.bitwise_xor(partner[0], place)
    values = lax.dot_general(
        node_feats, w_value, (((1,), (0,)), ((), ())), preferred_element_type=F32
    ).astype(BF16)
    key_vals = jnp.concatenate([key_vectors, values], 0)
    first = min(bits, GROUP_BITS)
    groups = []
    for shift in range(first, bits, GROUP_BITS):
        width = min(GROUP_BITS, bits - shift)
        number = jnp.bitwise_and(jnp.right_shift(match_mask, shift), (1 << width) - 1)
        groups.append((number, shift, 1 << width))
    masks = range(0 if groups else 1, 1 << first)
    number = jnp.bitwise_and(match_mask, (1 << first) - 1) - masks[0]
    moved = key_vals
    for group in groups:
        moved = route_group(moved, *group)
    outer, near, twin, inner, match = lax.switch(
        number, [partial(gather, mask) for mask in masks], key_vals, moved
    )
    out, dq, d_own, d_outer, d_near, d_twin, d_inner, d_match = attend(
        side, queries, out_grad, w_out, band_mask, expander_mask,
        key_vals, (outer, near, twin, inner, match),
    )
    twin, outer, inner, match = lax.switch(
        number, [partial(scatter, mask) for mask in masks],
        d_outer, d_near, d_twin, d_inner, d_match,
    )
    for group in groups:
        match = route_group(match, *group)
    dk, df = finish(w_value, d_own, (twin, outer, inner, match))
    return out, dq, dk, df


def solution(mesh):
    split = P("blk", None)
    return jax.shard_map(
        shards,
        mesh=mesh,
        in_specs=(split, split, split, P(), P(), split, split, P("blk"), split),
        out_specs=(split, split, split, split),
        check_vma=False,
    )
```
